32 devices in a mesh: member: 2 (over x), gx: 16 (over z, y, core).
Axes of the slice: x: 2, y: 2, z: 4, core: 2. Of those that a mesh axis runs over, the one named last changes fastest.
Arguments:
- fields: bfloat16 [5, 32, 64, 512], P(None, ('member', 'gx')), parts along dimension 1, may hold values from -6 to 6
- adjoint_seed: bfloat16 [5, 32, 64, 512], P(None, ('member', 'gx')), parts along dimension 1, may hold values from -6 to 6
- velocity: bfloat16 [3, 32, 64, 512], P(None, ('member', 'gx')), parts along dimension 1, may hold values from -6 to 6
- activity: int32 [32, 64], P(('member', 'gx')), parts along dimension 0, may hold values from 0 to 1, as said below
- diffusivity: float32 [5], replicated, may hold values from 0.05 to 0.5
- gram_cotangent: float32 [5, 5], replicated, may hold values from -262144 to 262144
Outputs:
- field_gradient: float32 [5, 32, 64, 512], P(None, ('member', 'gx')), parts along dimension 1
The draws below stay inside these ranges and needn't reach their ends.
There are 2 independent parts, one for each index of `member`. The reference program is written for one: setup_inputs(seed, part) draws one part's arguments, and reference() takes and returns one part's arrays. A program takes and returns all parts, laid end to end along the dimension named above; an argument that names none is the same for every part. Nothing has to cross between parts.
Inputs may be any that keep to these rules, and one draw needn't show every extreme that they name: `activity`: each layer holds at most 48 fluid elements and at least one; at least one layer holds exactly 48.
All inputs are finite; a program needn't handle non-finite values.
Results may differ from the reference program's by a relative error of at most 0.0054.
Values sent between devices are 32-bit elements; how exact they have to be, the bound alone decides.
A program may use at most 64 MiB of HBM per device.

```python
import math
import jax
import jax.numpy as jnp
import numpy as np
from jax import lax

FIELDS = 5
NODES = 512
EY = 4
EZ = 16
EX = 16
LIVE_MOST = 48


def draw_activity(key, part):
    key = jax.random.fold_in(key, 11)
    key_jitter, key_peak, key_perm = jax.random.split(key, 3)
    layer_ids = jnp.arange(EX, dtype=jnp.int32)
    baseline = LIVE_MOST // 3 + (LIVE_MOST - LIVE_MOST // 3) * layer_ids // max(EX - 1, 1)
    jitter = jax.random.randint(key_jitter, (EX,), 0, LIVE_MOST // 8 + 1)
    counts = jnp.maximum(baseline - jitter, 1)
    peak_layer = jax.random.randint(key_peak, (), 0, EX)
    counts = jnp.where(layer_ids == peak_layer, LIVE_MOST, counts)
    perm_keys = jax.random.split(key_perm, EX)
    ranks = jax.vmap(lambda subkey: jax.random.permutation(subkey, EY * EZ))(perm_keys)
    return (ranks < counts[:, None]).astype(jnp.int32)


def steps_of(key, extent, pieces, smallest, high):
    factor_of = 1.0
    for position, parts in pieces:
        draws = jax.random.uniform(jax.random.fold_in(jax.random.fold_in(key, 6), position), (parts,), jnp.float32, smallest / len(pieces), high / len(pieces))
        factor_of = factor_of * jnp.repeat(jnp.exp(draws), extent[position] // parts).reshape((-1,) + (1,) * (len(extent) - 1 - position))
    return factor_of


def noise(own_key, dims, width, limit, cuts=(), kind=jnp.bfloat16):
    values = width * jax.random.normal(own_key, dims, jnp.float32)
    if cuts:
        values = values * steps_of(own_key, dims, cuts, -0.22, 0.18)
    return jnp.clip(values, -limit, limit).astype(kind)


def setup_inputs(seed: int = 0, part: int = 0) -> dict:
    key_list = jax.random.split(jax.random.key(seed), 7)
    own_keys = jax.random.split(jax.random.fold_in(key_list[6], part), 7)
    fields = noise(own_keys[0], (FIELDS, EX, EY * EZ, NODES), 1.0, 6.0, ((1, 16),))
    adjoint_seed = noise(own_keys[1], (FIELDS, EX, EY * EZ, NODES), 1.0, 6.0, ((1, 16),))
    velocity = noise(own_keys[2], (3, EX, EY * EZ, NODES), 1.0, 6.0, ((1, 16),))
    activity = draw_activity(jax.random.fold_in(jax.random.fold_in(key_list[6], part), 71), part)
    diffusivity = jnp.clip(jnp.exp(jax.random.uniform(key_list[4], (FIELDS,), jnp.float32, math.log(0.05), math.log(0.5))), 0.05, 0.5)
    gram_cotangent = noise(key_list[5], (FIELDS, FIELDS), (40 * EX * EY * EZ), 262144.0, (), jnp.float32)
    return {"fields": fields, "adjoint_seed": adjoint_seed, "velocity": velocity, "activity": activity, "diffusivity": diffusivity, "gram_cotangent": gram_cotangent}


def basis_tables():
    degree = 7
    gll_points = np.array([-1.0, -0.8717401485096066, -0.5917001814331423, -0.2092992179024789,
                           0.2092992179024789, 0.5917001814331423, 0.8717401485096066, 1.0])
    prev_poly = np.ones(8)
    this_poly = gll_points.copy()
    for level in range(1, degree):
        prev_poly, this_poly = this_poly, ((2 * level + 1) * gll_points * this_poly - level * prev_poly) / (level + 1)
    gll_weights = 2.0 / (degree * (degree + 1) * this_poly ** 2)
    deriv = np.zeros((8, 8))
    for row_index in range(8):
        for col_index in range(8):
            if row_index != col_index:
                deriv[row_index, col_index] = this_poly[row_index] / (this_poly[col_index] * (gll_points[row_index] - gll_points[col_index]))
    deriv[0, 0] = -degree * (degree + 1) / 4.0
    deriv[7, 7] = degree * (degree + 1) / 4.0
    weight_cube = (gll_weights[:, None, None] * gll_weights[None, :, None] * gll_weights[None, None, :]).reshape(512)
    return weight_cube, deriv


def assemble(values, elem_dim, node_dim):
    moved = jnp.moveaxis(values, (elem_dim, node_dim), (0, 1))
    shared = moved[:-1, 7] + moved[1:, 0]
    moved = moved.at[:-1, 7].set(shared).at[1:, 0].set(shared)
    return jnp.moveaxis(moved, (0, 1), (elem_dim, node_dim))


def reference(fields, adjoint_seed, velocity, activity, diffusivity, gram_cotangent):
    weight_np, deriv_np = basis_tables()
    weight_cube = jnp.asarray(weight_np, jnp.float32)
    dmat = jnp.asarray(deriv_np, jnp.float32).astype(jnp.bfloat16).astype(jnp.float32)
    live = activity.astype(jnp.float32)
    high = lax.Precision.HIGHEST

    def layer(inputs):
        cotan, flow, field, mask = inputs
        adjoint = cotan.astype(jnp.float32)
        cube = adjoint.reshape(FIELDS, EY * EZ, 8, 8, 8)
        grad_a = jnp.einsum("ia,feabc->feibc", dmat, cube, precision=high).reshape(FIELDS, EY * EZ, NODES)
        grad_b = jnp.einsum("ib,feabc->feaic", dmat, cube, precision=high).reshape(FIELDS, EY * EZ, NODES)
        grad_c = jnp.einsum("ic,feabc->feabi", dmat, cube, precision=high).reshape(FIELDS, EY * EZ, NODES)
        grads = jnp.stack([grad_a, grad_b, grad_c], 0)
        flowf = flow.astype(jnp.float32)[:, None]
        coeff = diffusivity[None, :, None, None]
        fluxes = -(weight_cube * (flowf * adjoint[None] + coeff * grads))
        fluxes = lax.optimization_barrier(fluxes.astype(jnp.bfloat16)).astype(jnp.float32)
        fluxes = fluxes.reshape(3, FIELDS, EY * EZ, 8, 8, 8)
        back = jnp.einsum("ia,feibc->feabc", dmat, fluxes[0], precision=high)
        back = back + jnp.einsum("ib,feaic->feabc", dmat, fluxes[1], precision=high)
        back = back + jnp.einsum("ic,feabi->feabc", dmat, fluxes[2], precision=high)
        back = back.reshape(FIELDS, EY * EZ, NODES) * mask[None, :, None]
        fieldf = field.astype(jnp.float32)
        weighted = fieldf * weight_cube * mask[None, :, None]
        gram_part = jnp.einsum("fen,gen->fg", weighted, fieldf, precision=high)
        return back, gram_part

    inputs = (jnp.moveaxis(adjoint_seed, 1, 0), jnp.moveaxis(velocity, 1, 0), jnp.moveaxis(fields, 1, 0), live)
    backs, gram_parts = lax.map(layer, inputs)
    gram = jnp.sum(gram_parts, 0)
    trace = jnp.trace(gram)
    beta = jnp.sum(gram_cotangent * gram)
    gram_sym = (gram_cotangent + gram_cotangent.T) / 2.0
    fieldf = fields.astype(jnp.float32)
    mixed = jnp.einsum("fg,gxen->fxen", gram_sym, fieldf, precision=high)
    term = 2.0 * weight_cube * (mixed / trace - (beta / trace ** 2) * fieldf)
    local = (jnp.moveaxis(backs, 0, 1) + term) * live[None, :, :, None]
    grid = local.reshape(FIELDS, EX, EY, EZ, 8, 8, 8)
    grid = assemble(grid, 3, 6)
    grid = assemble(grid, 2, 5)
    grid = assemble(grid, 1, 4)
    return grid.reshape(FIELDS, EX, EY * EZ, NODES) * live[None, :, :, None]
```

```python
import functools
import jax
import jax.numpy as jnp
import ml_dtypes
import numpy as np
from jax import lax
from jax.experimental import pallas as pl
from jax.experimental.pallas import tpu as pltpu
from jax.sharding import PartitionSpec as P

EY = 4
EZ = 16
F32 = jnp.float32
BF16 = jnp.bfloat16


def basis_tables():
    degree = 7
    gll_points = np.array(
        [
            -1.0,
            -0.8717401485096066,
            -0.5917001814331423,
            -0.2092992179024789,
            0.2092992179024789,
            0.5917001814331423,
            0.8717401485096066,
            1.0,
        ]
    )
    prev_poly = np.ones(8)
    this_poly = gll_points.copy()
    for level in range(1, degree):
        prev_poly, this_poly = (
            this_poly,
            ((2 * level + 1) * gll_points * this_poly - level * prev_poly) / (level + 1),
        )
    gll_weights = 2.0 / (degree * (degree + 1) * this_poly**2)
    deriv = np.zeros((8, 8))
    for row_index in range(8):
        for col_index in range(8):
            if row_index != col_index:
                deriv[row_index, col_index] = this_poly[row_index] / (
                    this_poly[col_index] * (gll_points[row_index] - gll_points[col_index])
                )
    deriv[0, 0] = -degree * (degree + 1) / 4.0
    deriv[7, 7] = degree * (degree + 1) / 4.0
    weight_cube = (
        gll_weights[:, None, None] * gll_weights[None, :, None] * gll_weights[None, None, :]
    ).reshape(512)
    return (weight_cube, deriv)


def constants():
    weight_np, deriv_np = basis_tables()
    dmat = deriv_np.astype(np.float32).astype(ml_dtypes.bfloat16).astype(np.float32)
    eye = np.eye
    along_a = np.kron(dmat, eye(64))
    along_b = np.kron(eye(4), np.kron(dmat, eye(8)))
    along_c = np.kron(eye(32), dmat)
    faces = np.r_[0:64, 448:512]
    tables = (
        along_a.T,
        np.concatenate([along_b.T, along_c.T], 1),
        along_a,
        np.concatenate([along_b, along_c], 0),
        along_a[:, faces],
        np.concatenate([along_b[:128, :128], along_c[:128, :128]], 0),
    )
    tables = [np.ascontiguousarray(t).astype(ml_dtypes.bfloat16) for t in tables]
    weights = np.broadcast_to(weight_np.astype(np.float32)[None], (8, 512)).copy()
    return tables, weights


def kernel(
    n, nf, ne,
    diff, gram, act, fld_hbm, lam_hbm, vel_hbm, fa_hbm, fbc_hbm, ba_hbm, bbc_hbm, bfa_hbm, bfbc_hbm, w_hbm,
    out,
    fld, lam, vel, fa, fbc, ba, bbc, bfa, bfbc, wts,
    lw, q0, qbc, base, mixed, plain,
    part, parts, sbuf, rbuf,
    in_sem, psend, precv, fsend, frecv,
):
    me = lax.axis_index("gx")
    rows = nf * ne
    half = rows // 2

    pairs = (
        (fld_hbm, fld), (w_hbm, wts), (lam_hbm, lam), (fbc_hbm, fbc), (fa_hbm, fa), (vel_hbm, vel),
        (bfa_hbm, bfa), (bfbc_hbm, bfbc), (ba_hbm, ba), (bbc_hbm, bbc),
    )
    loads = [pltpu.make_async_copy(s, d, in_sem.at[i]) for i, (s, d) in enumerate(pairs)]
    for load in loads:
        load.start()
    l_fld, l_w, l_lam, l_fbc, l_fa, l_vel, l_bfa, l_bfbc, l_ba, l_bbc = loads

    barrier = pltpu.get_barrier_semaphore()

    @pl.loop(1, n)
    def _(o):
        pl.semaphore_signal(barrier, inc=1, device_id={"gx": lax.rem(me + o, n)}, device_id_type=pl.DeviceIdType.MESH)

    @pl.when(me == 0)
    def _():
        rbuf[0] = jnp.zeros((half, 128), F32)
        rbuf[2] = jnp.zeros((half, 128), F32)

    @pl.when(me == n - 1)
    def _():
        rbuf[1] = jnp.zeros((half, 128), F32)
        rbuf[3] = jnp.zeros((half, 128), F32)

    row = lax.broadcasted_iota(jnp.int32, (ne, 128), 0)
    lane = lax.broadcasted_iota(jnp.int32, (ne, 128), 1)
    low = lane < 64
    low_half = lax.broadcasted_iota(jnp.int32, (half, 128), 1) < 64
    c_id, b_id = lane & 7, (lane >> 3) & 7
    j_id, k_id = row >> 4, row & 15
    z_hi = (c_id == 7) & (k_id < EZ - 1)
    z_lo = (c_id == 0) & (k_id > 0)
    y_hi = (b_id == 7) & (j_id < EY - 1)
    y_lo = (b_id == 0) & (j_id > 0)

    def plane_sum(x):
        up, down = pltpu.roll(x, ne - 1, 0), pltpu.roll(x, 1, 0)
        x = x + jnp.where(z_hi, pltpu.roll(up, 7, 1), 0.0) + jnp.where(z_lo, pltpu.roll(down, 121, 1), 0.0)
        up = jnp.concatenate([x[EZ:], x[:EZ]], 0)
        down = jnp.concatenate([x[ne - EZ:], x[: ne - EZ]], 0)
        return x + jnp.where(y_hi, pltpu.roll(up, 56, 1), 0.0) + jnp.where(y_lo, pltpu.roll(down, 72, 1), 0.0)

    flag_row = jnp.broadcast_to(act[...].astype(F32), (ne, ne))
    diag = lax.broadcasted_iota(jnp.int32, (ne, ne), 0) == lax.broadcasted_iota(jnp.int32, (ne, ne), 1)
    mask = jnp.dot(
        jnp.where(diag, flag_row, 0.0).astype(BF16), jnp.ones((ne, 128), BF16), preferred_element_type=F32
    )
    sym = [[(gram[f, h] + gram[h, f]) * 0.5 for h in range(nf)] for f in range(nf)]

    l_fld.wait()
    l_w.wait()
    t_acc = jnp.zeros((8, 128), F32)
    b_acc = jnp.zeros((8, 128), F32)
    for ct in range(4):
        cols = slice(ct * 128, ct * 128 + 128)
        u = [fld[f * ne:(f + 1) * ne, cols].astype(F32) for f in range(nf)]
        square = sum(x * x for x in u)
        quad = 0.0
        for f in range(nf):
            inner = sym[f][f] * u[f]
            for h in range(f + 1, nf):
                inner = inner + (2.0 * sym[f][h]) * u[h]
            quad = quad + u[f] * inner
        mw = mask * wts[0:1, cols]
        t_acc = t_acc + jnp.sum((mw * square).reshape(ne // 8, 8, 128), 0)
        b_acc = b_acc + jnp.sum((mw * quad).reshape(ne // 8, 8, 128), 0)
    part[0:8] = t_acc
    part[8:16] = b_acc

    pl.semaphore_wait(barrier, n - 1)

    @pl.loop(1, n)
    def _(o):
        pltpu.make_async_remote_copy(
            src_ref=part, dst_ref=parts.at[o - 1], send_sem=psend.at[o - 1], recv_sem=precv.at[o - 1],
            device_id={"gx": lax.rem(me + o, n)}, device_id_type=pl.DeviceIdType.MESH,
        ).start()

    def face_copy(slot):
        target = me - 1 if slot % 2 == 0 else me + 1
        there = slot + 1 if slot % 2 == 0 else slot - 1
        return pltpu.make_async_remote_copy(
            src_ref=sbuf.at[slot], dst_ref=rbuf.at[there], send_sem=fsend.at[slot], recv_sem=frecv.at[there],
            device_id={"gx": target}, device_id_type=pl.DeviceIdType.MESH,
        )

    def pack(face, slot):
        a, b = face[:half], face[half:]
        sbuf[slot] = jnp.where(low_half, a, pltpu.roll(b, 64, 1))
        sbuf[slot + 1] = jnp.where(low_half, pltpu.roll(a, 64, 1), b)

        @pl.when(me > 0)
        def _():
            face_copy(slot).start()

        @pl.when(me < n - 1)
        def _():
            face_copy(slot + 1).start()

    def unpack(slot):
        p, q = rbuf[slot], rbuf[slot + 1]
        return jnp.concatenate(
            [jnp.where(low_half, p, pltpu.roll(q, 64, 1)), jnp.where(low_half, pltpu.roll(p, 64, 1), q)], 0
        )

    def done(slot):
        @pl.when(me > 0)
        def _():
            face_copy(slot).wait_send()
            pltpu.make_async_copy(rbuf.at[slot], rbuf.at[slot], frecv.at[slot]).wait()

        @pl.when(me < n - 1)
        def _():
            face_copy(slot + 1).wait_send()
            pltpu.make_async_copy(rbuf.at[slot + 1], rbuf.at[slot + 1], frecv.at[slot + 1]).wait()

    pack(
        jnp.concatenate(
            [
                plane_sum(
                    mask
                    * jnp.where(
                        low, fld[f * ne:(f + 1) * ne, 0:128].astype(F32), fld[f * ne:(f + 1) * ne, 384:512].astype(F32)
                    )
                )
                for f in range(nf)
            ],
            0,
        ),
        0,
    )

    l_lam.wait()
    for f in range(nf):
        rs = slice(f * ne, (f + 1) * ne)
        lw[rs] = -wts[0:1] * lam[rs].astype(F32)
    l_fbc.wait()
    l_fa.wait()
    l_vel.wait()
    for d in range(3):
        for t in range(2):
            cols = slice(t * 256, t * 256 + 256)
            if d == 0:
                grad = jnp.dot(lam[...], fa[:, cols], preferred_element_type=F32)
            else:
                grad = jnp.dot(lam[:, cols], fbc[:, (d - 1) * 256:d * 256], preferred_element_type=F32)
            flow = vel[d * ne:(d + 1) * ne, cols].astype(F32)
            for f in range(nf):
                rs = slice(f * ne, (f + 1) * ne)
                flux = (lw[rs, cols] * flow - (diff[f] * wts[0:1, cols]) * grad[rs]).astype(BF16)
                if d == 0:
                    q0[rs, cols] = flux
                else:
                    qbc[t, rs, (d - 1) * 256:d * 256] = flux

    l_bfa.wait()
    l_bfbc.wait()
    low_rows = lax.broadcasted_iota(jnp.int32, (rows, 128), 1) < 64
    q1f = jnp.where(low_rows, qbc[0, :, 0:128], qbc[1, :, 128:256])
    q2f = jnp.where(low_rows, qbc[0, :, 256:384], qbc[1, :, 384:512])
    face = jnp.dot(q0[...], bfa[...], preferred_element_type=F32) + jnp.dot(
        jnp.concatenate([q1f, q2f], 1), bfbc[...], preferred_element_type=F32
    )
    pack(jnp.concatenate([plane_sum(mask * face[f * ne:(f + 1) * ne]) for f in range(nf)], 0), 2)

    l_ba.wait()
    l_bbc.wait()
    for t in range(2):
        cols = slice(t * 256, t * 256 + 256)
        back = jnp.dot(q0[...], ba[:, cols], preferred_element_type=F32) + jnp.dot(
            qbc[t], bbc[...], preferred_element_type=F32
        )
        for s in range(2):
            ct = slice(t * 256 + s * 128, t * 256 + s * 128 + 128)
            for f in range(nf):
                rs = slice(f * ne, (f + 1) * ne)
                base[rs, ct] = mask * plane_sum(mask * back[rs, s * 128:s * 128 + 128])
    for ct in range(4):
        cols = slice(ct * 128, ct * 128 + 128)
        mw = mask * wts[0:1, cols]
        u = [mw * plane_sum(mask * fld[f * ne:(f + 1) * ne, cols].astype(F32)) for f in range(nf)]
        for f in range(nf):
            rs = slice(f * ne, (f + 1) * ne)
            plain[rs, cols] = u[f]
            mixed[rs, cols] = sum(sym[f][h] * u[h] for h in range(nf))

    for o in range(1, n):
        copy = pltpu.make_async_remote_copy(
            src_ref=part, dst_ref=parts.at[o - 1], send_sem=psend.at[o - 1], recv_sem=precv.at[o - 1],
            device_id={"gx": lax.rem(me + o, n)}, device_id_type=pl.DeviceIdType.MESH,
        )
        copy.wait()
    total = part[...] + jnp.sum(parts[...], 0)
    trace = jnp.sum(total[0:8], keepdims=True)
    beta = jnp.sum(total[8:16], keepdims=True)
    c1 = jnp.broadcast_to(2.0 / trace, (1, 128))
    c2 = jnp.broadcast_to(-2.0 * beta / (trace * trace), (1, 128))
    for ct in (1, 2):
        cols = slice(ct * 128, ct * 128 + 128)
        out[:, cols] = base[:, cols] + c1 * mixed[:, cols] + c2 * plain[:, cols]

    done(0)
    got = unpack(0)
    wf = mask * jnp.where(low, wts[0:1, 0:128], wts[0:1, 384:512])
    u = [wf * got[f * ne:(f + 1) * ne] for f in range(nf)]
    extra = [c1 * sum(sym[f][h] * u[h] for h in range(nf)) + c2 * u[f] for f in range(nf)]
    for ct in (0, 3):
        cols = slice(ct * 128, ct * 128 + 128)
        for f in range(nf):
            rs = slice(f * ne, (f + 1) * ne)
            side = low if ct == 0 else ~low
            base[rs, cols] = (
                base[rs, cols] + c1 * mixed[rs, cols] + c2 * plain[rs, cols] + jnp.where(side, extra[f], 0.0)
            )
    done(2)
    got = unpack(2)
    for ct in (0, 3):
        cols = slice(ct * 128, ct * 128 + 128)
        for f in range(nf):
            rs = slice(f * ne, (f + 1) * ne)
            side = low if ct == 0 else ~low
            out[rs, cols] = base[rs, cols] + jnp.where(side, mask * got[rs], 0.0)


def per_device(n, fields, adjoint_seed, velocity, activity, diffusivity, gram_cotangent):
    nf, _, ne, nn = fields.shape
    rows = nf * ne
    tables, weights = constants()
    vmem, anywhere = pl.BlockSpec(memory_space=pltpu.VMEM), pl.BlockSpec(memory_space=pl.ANY)
    smem = pl.BlockSpec(memory_space=pltpu.SMEM)
    result = pl.pallas_call(
        functools.partial(kernel, n, nf, ne),
        out_shape=jax.ShapeDtypeStruct((rows, nn), F32),
        in_specs=[smem, smem, vmem] + [anywhere] * 10,
        out_specs=vmem,
        scratch_shapes=[
            pltpu.VMEM((rows, nn), BF16),
            pltpu.VMEM((rows, nn), BF16),
            pltpu.VMEM((3 * ne, nn), BF16),
            *[pltpu.VMEM(t.shape, BF16) for t in tables],
            pltpu.VMEM((8, nn), F32),
            pltpu.VMEM((rows, nn), F32),
            pltpu.VMEM((rows, nn), BF16),
            pltpu.VMEM((2, rows, nn), BF16),
            pltpu.VMEM((rows, nn), F32),
            pltpu.VMEM((rows, nn), F32),
            pltpu.VMEM((rows, nn), F32),
            pltpu.VMEM((16, 128), F32),
            pltpu.VMEM((n - 1, 16, 128), F32),
            pltpu.VMEM((4, rows // 2, 128), F32),
            pltpu.VMEM((4, rows // 2, 128), F32),
            pltpu.SemaphoreType.DMA((10,)),
            pltpu.SemaphoreType.DMA((n - 1,)),
            pltpu.SemaphoreType.DMA((n - 1,)),
            pltpu.SemaphoreType.DMA((4,)),
            pltpu.SemaphoreType.DMA((4,)),
        ],
        compiler_params=pltpu.CompilerParams(
            collective_id=0, has_side_effects=True, vmem_limit_bytes=32 * 1024 * 1024
        ),
    )(
        diffusivity,
        gram_cotangent,
        activity,
        fields.reshape(rows, nn),
        adjoint_seed.reshape(rows, nn),
        velocity.reshape(3 * ne, nn),
        *[jnp.asarray(t) for t in tables],
        jnp.asarray(weights),
    )
    return result.reshape(nf, 1, ne, nn)


def solution(mesh):
    spec = P(None, ("member", "gx"), None, None)
    return jax.shard_map(
        functools.partial(per_device, mesh.shape["gx"]),
        mesh=mesh,
        in_specs=(spec, spec, spec, P(("member", "gx"), None), P(), P()),
        out_specs=spec,
        check_vma=False,
    )
```

```python
import functools
import jax
import jax.numpy as jnp
import ml_dtypes
import numpy as np
from jax import lax
from jax.experimental import pallas as pl
from jax.experimental.pallas import tpu as pltpu
from jax.sharding import PartitionSpec as P

EY = 4
EZ = 16
F32 = jnp.float32
BF16 = jnp.bfloat16


def basis_tables():
    degree = 7
    gll_points = np.array(
        [
            -1.0,
            -0.8717401485096066,
            -0.5917001814331423,
            -0.2092992179024789,
            0.2092992179024789,
            0.5917001814331423,
            0.8717401485096066,
            1.0,
        ]
    )
    prev_poly = np.ones(8)
    this_poly = gll_points.copy()
    for level in range(1, degree):
        prev_poly, this_poly = (
            this_poly,
            ((2 * level + 1) * gll_points * this_poly - level * prev_poly) / (level + 1),
        )
    gll_weights = 2.0 / (degree * (degree + 1) * this_poly**2)
    deriv = np.zeros((8, 8))
    for row_index in range(8):
        for col_index in range(8):
            if row_index != col_index:
                deriv[row_index, col_index] = this_poly[row_index] / (
                    this_poly[col_index] * (gll_points[row_index] - gll_points[col_index])
                )
    deriv[0, 0] = -degree * (degree + 1) / 4.0
    deriv[7, 7] = degree * (degree + 1) / 4.0
    weight_cube = (
        gll_weights[:, None, None] * gll_weights[None, :, None] * gll_weights[None, None, :]
    ).reshape(512)
    return (weight_cube, deriv)


def constants():
    weight_np, deriv_np = basis_tables()
    dmat = deriv_np.astype(np.float32).astype(ml_dtypes.bfloat16).astype(np.float32)
    lanes = np.arange(512)
    pieces = []
    for index in (lanes // 64, (lanes[:128] // 8) % 8, lanes[:128] % 8):
        pieces += [dmat[:, index], dmat.T[:, index]]
    pieces.append(np.broadcast_to(weight_np.astype(np.float32)[None], (8, 512)))
    return np.ascontiguousarray(np.concatenate(pieces, 1).astype(np.float32))


def build_tables(spread, fa, fbc, ba, bbc, bfa, bfbc):
    row64 = lax.broadcasted_iota(jnp.int32, (64, 512), 0)
    lane64 = lax.broadcasted_iota(jnp.int32, (64, 512), 1) & 63
    same = row64 == lane64
    low = lax.broadcasted_iota(jnp.int32, (64, 128), 1) < 64
    for p in range(8):
        rs = slice(p * 64, p * 64 + 64)
        plain = jnp.where(same, spread[p:p + 1, 0:512], 0.0).astype(BF16)
        ba[rs] = plain
        bfa[rs] = jnp.where(low, plain[:, 0:128], plain[:, 384:512])
        fa[rs] = jnp.where(same, spread[p:p + 1, 512:1024], 0.0).astype(BF16)
    row = lax.broadcasted_iota(jnp.int32, (128, 128), 0)
    lane = lax.broadcasted_iota(jnp.int32, (128, 128), 1)
    b_same = ((row & 7) == (lane & 7)) & ((row >> 6) == (lane >> 6))
    c_same = (row >> 3) == (lane >> 3)

    def b_table(at):
        rows = [jnp.broadcast_to(spread[g % 8:g % 8 + 1, at:at + 128], (8, 128)) for g in range(16)]
        return jnp.where(b_same, jnp.concatenate(rows, 0), 0.0).astype(BF16)

    def c_table(at):
        return jnp.where(c_same, jnp.concatenate([spread[:, at:at + 128]] * 16, 0), 0.0).astype(BF16)

    zero = jnp.zeros((128, 128), BF16)
    b, bt, c, ct = b_table(1024), b_table(1152), c_table(1280), c_table(1408)
    for k, (back, fwd) in enumerate(((b, bt), (c, ct))):
        fbc[0:128, k * 256:k * 256 + 256] = jnp.concatenate([fwd, zero], 1)
        fbc[128:256, k * 256:k * 256 + 256] = jnp.concatenate([zero, fwd], 1)
        bbc[k * 256:k * 256 + 128] = jnp.concatenate([back, zero], 1)
        bbc[k * 256 + 128:k * 256 + 256] = jnp.concatenate([zero, back], 1)
        bfbc[k * 128:k * 128 + 128] = back


def kernel(
    n, nf, ne,
    diff, gram, act, fld_hbm, lam_hbm, vel_hbm, spread_hbm,
    out,
    fld, lam, vel, fa, fbc, ba, bbc, bfa, bfbc, spread,
    lw, q0, qbc, base, mixed, plain,
    part, parts, sbuf, rbuf,
    in_sem, psend, precv, fsend, frecv,
):
    me = lax.axis_index("gx")
    rows = nf * ne
    half = rows // 2

    pairs = ((spread_hbm, spread), (fld_hbm, fld), (lam_hbm, lam), (vel_hbm, vel))
    loads = [pltpu.make_async_copy(s, d, in_sem.at[i]) for i, (s, d) in enumerate(pairs)]
    for load in loads:
        load.start()
    l_spread, l_fld, l_lam, l_vel = loads

    barrier = pltpu.get_barrier_semaphore()

    @pl.loop(1, n)
    def _(o):
        pl.semaphore_signal(barrier, inc=1, device_id={"gx": lax.rem(me + o, n)}, device_id_type=pl.DeviceIdType.MESH)

    @pl.when(me == 0)
    def _():
        rbuf[0] = jnp.zeros((half, 128), F32)
        rbuf[2] = jnp.zeros((half, 128), F32)

    @pl.when(me == n - 1)
    def _():
        rbuf[1] = jnp.zeros((half, 128), F32)
        rbuf[3] = jnp.zeros((half, 128), F32)

    row = lax.broadcasted_iota(jnp.int32, (ne, 128), 0)
    lane = lax.broadcasted_iota(jnp.int32, (ne, 128), 1)
    low = lane < 64
    low_half = lax.broadcasted_iota(jnp.int32, (half, 128), 1) < 64
    c_id, b_id = lane & 7, (lane >> 3) & 7
    j_id, k_id = row >> 4, row & 15
    z_hi = (c_id == 7) & (k_id < EZ - 1)
    z_lo = (c_id == 0) & (k_id > 0)
    y_hi = (b_id == 7) & (j_id < EY - 1)
    y_lo = (b_id == 0) & (j_id > 0)

    def plane_sum(x):
        up, down = pltpu.roll(x, ne - 1, 0), pltpu.roll(x, 1, 0)
        x = x + jnp.where(z_hi, pltpu.roll(up, 7, 1), 0.0) + jnp.where(z_lo, pltpu.roll(down, 121, 1), 0.0)
        up = jnp.concatenate([x[EZ:], x[:EZ]], 0)
        down = jnp.concatenate([x[ne - EZ:], x[: ne - EZ]], 0)
        return x + jnp.where(y_hi, pltpu.roll(up, 56, 1), 0.0) + jnp.where(y_lo, pltpu.roll(down, 72, 1), 0.0)

    flag_row = jnp.broadcast_to(act[...].astype(F32), (ne, ne))
    diag = lax.broadcasted_iota(jnp.int32, (ne, ne), 0) == lax.broadcasted_iota(jnp.int32, (ne, ne), 1)
    mask = jnp.dot(
        jnp.where(diag, flag_row, 0.0).astype(BF16), jnp.ones((ne, 128), BF16), preferred_element_type=F32
    )
    sym = [[(gram[f, h] + gram[h, f]) * 0.5 for h in range(nf)] for f in range(nf)]

    l_spread.wait()
    wts = spread[0:8, 1536:2048]
    build_tables(spread, fa, fbc, ba, bbc, bfa, bfbc)
    l_fld.wait()
    t_acc = jnp.zeros((8, 128), F32)
    b_acc = jnp.zeros((8, 128), F32)
    for ct in range(4):
        cols = slice(ct * 128, ct * 128 + 128)
        u = [fld[f * ne:(f + 1) * ne, cols].astype(F32) for f in range(nf)]
        square = sum(x * x for x in u)
        quad = 0.0
        for f in range(nf):
            inner = sym[f][f] * u[f]
            for h in range(f + 1, nf):
                inner = inner + (2.0 * sym[f][h]) * u[h]
            quad = quad + u[f] * inner
        mw = mask * wts[0:1, cols]
        t_acc = t_acc + jnp.sum((mw * square).reshape(ne // 8, 8, 128), 0)
        b_acc = b_acc + jnp.sum((mw * quad).reshape(ne // 8, 8, 128), 0)
    part[0:8] = t_acc
    part[8:16] = b_acc

    pl.semaphore_wait(barrier, n - 1)

    @pl.loop(1, n)
    def _(o):
        pltpu.make_async_remote_copy(
            src_ref=part, dst_ref=parts.at[o - 1], send_sem=psend.at[o - 1], recv_sem=precv.at[o - 1],
            device_id={"gx": lax.rem(me + o, n)}, device_id_type=pl.DeviceIdType.MESH,
        ).start()

    def face_copy(slot):
        target = me - 1 if slot % 2 == 0 else me + 1
        there = slot + 1 if slot % 2 == 0 else slot - 1
        return pltpu.make_async_remote_copy(
            src_ref=sbuf.at[slot], dst_ref=rbuf.at[there], send_sem=fsend.at[slot], recv_sem=frecv.at[there],
            device_id={"gx": target}, device_id_type=pl.DeviceIdType.MESH,
        )

    def pack(face, slot):
        a, b = face[:half], face[half:]
        sbuf[slot] = jnp.where(low_half, a, pltpu.roll(b, 64, 1))
        sbuf[slot + 1] = jnp.where(low_half, pltpu.roll(a, 64, 1), b)

        @pl.when(me > 0)
        def _():
            face_copy(slot).start()

        @pl.when(me < n - 1)
        def _():
            face_copy(slot + 1).start()

    def unpack(slot):
        p, q = rbuf[slot], rbuf[slot + 1]
        return jnp.concatenate(
            [jnp.where(low_half, p, pltpu.roll(q, 64, 1)), jnp.where(low_half, pltpu.roll(p, 64, 1), q)], 0
        )

    def done(slot):
        @pl.when(me > 0)
        def _():
            face_copy(slot).wait_send()
            pltpu.make_async_copy(rbuf.at[slot], rbuf.at[slot], frecv.at[slot]).wait()

        @pl.when(me < n - 1)
        def _():
            face_copy(slot + 1).wait_send()
            pltpu.make_async_copy(rbuf.at[slot + 1], rbuf.at[slot + 1], frecv.at[slot + 1]).wait()

    pack(
        jnp.concatenate(
            [
                plane_sum(
                    mask
                    * jnp.where(
                        low, fld[f * ne:(f + 1) * ne, 0:128].astype(F32), fld[f * ne:(f + 1) * ne, 384:512].astype(F32)
                    )
                )
                for f in range(nf)
            ],
            0,
        ),
        0,
    )

    l_lam.wait()
    for f in range(nf):
        rs = slice(f * ne, (f + 1) * ne)
        lw[rs] = -wts[0:1] * lam[rs].astype(F32)
    l_vel.wait()
    for d in range(3):
        for t in range(2):
            cols = slice(t * 256, t * 256 + 256)
            if d == 0:
                grad = jnp.dot(lam[...], fa[:, cols], preferred_element_type=F32)
            else:
                grad = jnp.dot(lam[:, cols], fbc[:, (d - 1) * 256:d * 256], preferred_element_type=F32)
            flow = vel[d * ne:(d + 1) * ne, cols].astype(F32)
            for f in range(nf):
                rs = slice(f * ne, (f + 1) * ne)
                flux = (lw[rs, cols] * flow - (diff[f] * wts[0:1, cols]) * grad[rs]).astype(BF16)
                if d == 0:
                    q0[rs, cols] = flux
                else:
                    qbc[t, rs, (d - 1) * 256:d * 256] = flux

    low_rows = lax.broadcasted_iota(jnp.int32, (rows, 128), 1) < 64
    q1f = jnp.where(low_rows, qbc[0, :, 0:128], qbc[1, :, 128:256])
    q2f = jnp.where(low_rows, qbc[0, :, 256:384], qbc[1, :, 384:512])
    face = jnp.dot(q0[...], bfa[...], preferred_element_type=F32) + jnp.dot(
        jnp.concatenate([q1f, q2f], 1), bfbc[...], preferred_element_type=F32
    )
    pack(jnp.concatenate([plane_sum(mask * face[f * ne:(f + 1) * ne]) for f in range(nf)], 0), 2)

    for t in range(2):
        cols = slice(t * 256, t * 256 + 256)
        back = jnp.dot(q0[...], ba[:, cols], preferred_element_type=F32) + jnp.dot(
            qbc[t], bbc[...], preferred_element_type=F32
        )
        for s in range(2):
            ct = slice(t * 256 + s * 128, t * 256 + s * 128 + 128)
            for f in range(nf):
                rs = slice(f * ne, (f + 1) * ne)
                base[rs, ct] = mask * plane_sum(mask * back[rs, s * 128:s * 128 + 128])
    for ct in range(4):
        cols = slice(ct * 128, ct * 128 + 128)
        mw = mask * wts[0:1, cols]
        u = [mw * plane_sum(mask * fld[f * ne:(f + 1) * ne, cols].astype(F32)) for f in range(nf)]
        for f in range(nf):
            rs = slice(f * ne, (f + 1) * ne)
            plain[rs, cols] = u[f]
            mixed[rs, cols] = sum(sym[f][h] * u[h] for h in range(nf))

    for o in range(1, n):
        copy = pltpu.make_async_remote_copy(
            src_ref=part, dst_ref=parts.at[o - 1], send_sem=psend.at[o - 1], recv_sem=precv.at[o - 1],
            device_id={"gx": lax.rem(me + o, n)}, device_id_type=pl.DeviceIdType.MESH,
        )
        copy.wait()
    total = part[...] + jnp.sum(parts[...], 0)
    trace = jnp.sum(total[0:8], keepdims=True)
    beta = jnp.sum(total[8:16], keepdims=True)
    c1 = jnp.broadcast_to(2.0 / trace, (1, 128))
    c2 = jnp.broadcast_to(-2.0 * beta / (trace * trace), (1, 128))
    for ct in (1, 2):
        cols = slice(ct * 128, ct * 128 + 128)
        out[:, cols] = base[:, cols] + c1 * mixed[:, cols] + c2 * plain[:, cols]

    done(0)
    got = unpack(0)
    wf = mask * jnp.where(low, wts[0:1, 0:128], wts[0:1, 384:512])
    u = [wf * got[f * ne:(f + 1) * ne] for f in range(nf)]
    extra = [c1 * sum(sym[f][h] * u[h] for h in range(nf)) + c2 * u[f] for f in range(nf)]
    for ct in (0, 3):
        cols = slice(ct * 128, ct * 128 + 128)
        for f in range(nf):
            rs = slice(f * ne, (f + 1) * ne)
            side = low if ct == 0 else ~low
            base[rs, cols] = (
                base[rs, cols] + c1 * mixed[rs, cols] + c2 * plain[rs, cols] + jnp.where(side, extra[f], 0.0)
            )
    done(2)
    got = unpack(2)
    for ct in (0, 3):
        cols = slice(ct * 128, ct * 128 + 128)
        for f in range(nf):
            rs = slice(f * ne, (f + 1) * ne)
            side = low if ct == 0 else ~low
            out[rs, cols] = base[rs, cols] + jnp.where(side, mask * got[rs], 0.0)


def per_device(n, fields, adjoint_seed, velocity, activity, diffusivity, gram_cotangent):
    nf, _, ne, nn = fields.shape
    rows = nf * ne
    table_shapes = ((nn, nn), (256, 512), (nn, nn), (512, 256), (nn, 128), (256, 128))
    vmem, anywhere = pl.BlockSpec(memory_space=pltpu.VMEM), pl.BlockSpec(memory_space=pltpu.HBM)
    smem = pl.BlockSpec(memory_space=pltpu.SMEM)
    result = pl.pallas_call(
        functools.partial(kernel, n, nf, ne),
        out_shape=pltpu.VMEM((rows, nn), F32),
        in_specs=[smem, smem, vmem] + [anywhere] * 4,
        out_specs=vmem,
        scratch_shapes=[
            pltpu.VMEM((rows, nn), BF16),
            pltpu.VMEM((rows, nn), BF16),
            pltpu.VMEM((3 * ne, nn), BF16),
            *[pltpu.VMEM(t, BF16) for t in table_shapes],
            pltpu.VMEM((8, 1536 + nn), F32),
            pltpu.VMEM((rows, nn), F32),
            pltpu.VMEM((rows, nn), BF16),
            pltpu.VMEM((2, rows, nn), BF16),
            pltpu.VMEM((rows, nn), F32),
            pltpu.VMEM((rows, nn), F32),
            pltpu.VMEM((rows, nn), F32),
            pltpu.VMEM((16, 128), F32),
            pltpu.VMEM((n - 1, 16, 128), F32),
            pltpu.VMEM((4, rows // 2, 128), F32),
            pltpu.VMEM((4, rows // 2, 128), F32),
            pltpu.SemaphoreType.DMA((4,)),
            pltpu.SemaphoreType.DMA((n - 1,)),
            pltpu.SemaphoreType.DMA((n - 1,)),
            pltpu.SemaphoreType.DMA((4,)),
            pltpu.SemaphoreType.DMA((4,)),
        ],
        compiler_params=pltpu.CompilerParams(
            collective_id=0, has_side_effects=True, vmem_limit_bytes=60 * 1024 * 1024
        ),
    )(
        diffusivity,
        gram_cotangent,
        activity,
        fields.reshape(rows, nn),
        adjoint_seed.reshape(rows, nn),
        velocity.reshape(3 * ne, nn),
        jnp.asarray(constants()),
    )
    return result.reshape(nf, 1, ne, nn)


def solution(mesh):
    spec = P(None, ("member", "gx"), None, None)
    return jax.shard_map(
        functools.partial(per_device, mesh.shape["gx"]),
        mesh=mesh,
        in_specs=(spec, spec, spec, P(("member", "gx"), None), P(), P()),
        out_specs=spec,
        check_vma=False,
    )
```

```python
import functools
import jax
import jax.numpy as jnp
import ml_dtypes
import numpy as np
from jax import lax
from jax.experimental import pallas as pl
from jax.experimental.pallas import tpu as pltpu
from jax.sharding import PartitionSpec as P

EY = 4
EZ = 16
F32 = jnp.float32
BF16 = jnp.bfloat16


def basis_tables():
    degree = 7
    gll_points = np.array(
        [
            -1.0,
            -0.8717401485096066,
            -0.5917001814331423,
            -0.2092992179024789,
            0.2092992179024789,
            0.5917001814331423,
            0.8717401485096066,
            1.0,
        ]
    )
    prev_poly = np.ones(8)
    this_poly = gll_points.copy()
    for level in range(1, degree):
        prev_poly, this_poly = (
            this_poly,
            ((2 * level + 1) * gll_points * this_poly - level * prev_poly) / (level + 1),
        )
    gll_weights = 2.0 / (degree * (degree + 1) * this_poly**2)
    deriv = np.zeros((8, 8))
    for row_index in range(8):
        for col_index in range(8):
            if row_index != col_index:
                deriv[row_index, col_index] = this_poly[row_index] / (
                    this_poly[col_index] * (gll_points[row_index] - gll_points[col_index])
                )
    deriv[0, 0] = -degree * (degree + 1) / 4.0
    deriv[7, 7] = degree * (degree + 1) / 4.0
    weight_cube = (
        gll_weights[:, None, None] * gll_weights[None, :, None] * gll_weights[None, None, :]
    ).reshape(512)
    return (weight_cube, deriv)


def constants():
    weight_np, deriv_np = basis_tables()
    dmat = deriv_np.astype(np.float32).astype(ml_dtypes.bfloat16).astype(np.float32)
    lanes = np.arange(512)
    pieces = []
    for index in (lanes // 64, (lanes[:128] // 8) % 8, lanes[:128] % 8):
        pieces += [dmat[:, index], dmat.T[:, index]]
    pieces.append(np.broadcast_to(weight_np.astype(np.float32)[None], (8, 512)))
    return np.ascontiguousarray(np.concatenate(pieces, 1).astype(np.float32))


def build_tables(spread, fa, fbc, ba, bbc, bfa, bfbc):
    row64 = lax.broadcasted_iota(jnp.int32, (64, 512), 0)
    lane64 = lax.broadcasted_iota(jnp.int32, (64, 512), 1) & 63
    same = row64 == lane64
    low = lax.broadcasted_iota(jnp.int32, (64, 128), 1) < 64
    for p in range(8):
        rs = slice(p * 64, p * 64 + 64)
        plain = jnp.where(same, spread[p:p + 1, 0:512], 0.0).astype(BF16)
        ba[rs] = plain
        bfa[rs] = jnp.where(low, plain[:, 0:128], plain[:, 384:512])
        fa[rs] = jnp.where(same, spread[p:p + 1, 512:1024], 0.0).astype(BF16)
    row = lax.broadcasted_iota(jnp.int32, (128, 128), 0)
    lane = lax.broadcasted_iota(jnp.int32, (128, 128), 1)
    b_same = ((row & 7) == (lane & 7)) & ((row >> 6) == (lane >> 6))
    c_same = (row >> 3) == (lane >> 3)

    def b_table(at):
        rows = [jnp.broadcast_to(spread[g % 8:g % 8 + 1, at:at + 128], (8, 128)) for g in range(16)]
        return jnp.where(b_same, jnp.concatenate(rows, 0), 0.0).astype(BF16)

    def c_table(at):
        return jnp.where(c_same, jnp.concatenate([spread[:, at:at + 128]] * 16, 0), 0.0).astype(BF16)

    zero = jnp.zeros((128, 128), BF16)
    b, bt, c, ct = b_table(1024), b_table(1152), c_table(1280), c_table(1408)
    for k, (back, fwd) in enumerate(((b, bt), (c, ct))):
        fbc[0:128, k * 256:k * 256 + 256] = jnp.concatenate([fwd, zero], 1)
        fbc[128:256, k * 256:k * 256 + 256] = jnp.concatenate([zero, fwd], 1)
        bbc[k * 256:k * 256 + 128] = jnp.concatenate([back, zero], 1)
        bbc[k * 256 + 128:k * 256 + 256] = jnp.concatenate([zero, back], 1)
        bfbc[k * 128:k * 128 + 128] = back


def kernel(
    n, nf, ne,
    diff, gram, act, fld_hbm, lam_hbm, vel_hbm, spread_hbm,
    out,
    fld, lam, vel, fa, fbc, ba, bbc, bfa, bfbc, spread,
    lw, q0, qbc, base, mixed, plain, ends,
    part, parts, sbuf, rbuf,
    in_sem, psend, precv, fsend, frecv,
):
    me = lax.axis_index("gx")
    rows = nf * ne
    half = rows // 2

    pairs = ((spread_hbm, spread), (fld_hbm, fld), (lam_hbm, lam), (vel_hbm, vel))
    loads = [pltpu.make_async_copy(s, d, in_sem.at[i]) for i, (s, d) in enumerate(pairs)]
    for load in loads:
        load.start()
    l_spread, l_fld, l_lam, l_vel = loads

    barrier = pltpu.get_barrier_semaphore()

    @pl.loop(1, n)
    def _(o):
        pl.semaphore_signal(barrier, inc=1, device_id={"gx": lax.rem(me + o, n)}, device_id_type=pl.DeviceIdType.MESH)

    @pl.when(me == 0)
    def _():
        rbuf[0] = jnp.zeros((half, 128), F32)
        rbuf[2] = jnp.zeros((half, 128), F32)

    @pl.when(me == n - 1)
    def _():
        rbuf[1] = jnp.zeros((half, 128), F32)
        rbuf[3] = jnp.zeros((half, 128), F32)

    row = lax.broadcasted_iota(jnp.int32, (ne, 128), 0)
    lane = lax.broadcasted_iota(jnp.int32, (ne, 128), 1)
    low = lane < 64
    low_half = lax.broadcasted_iota(jnp.int32, (half, 128), 1) < 64
    c_id, b_id = lane & 7, (lane >> 3) & 7
    j_id, k_id = row >> 4, row & 15
    z_hi = (c_id == 7) & (k_id < EZ - 1)
    z_lo = (c_id == 0) & (k_id > 0)
    y_hi = (b_id == 7) & (j_id < EY - 1)
    y_lo = (b_id == 0) & (j_id > 0)

    def plane_sum(x):
        up, down = pltpu.roll(x, ne - 1, 0), pltpu.roll(x, 1, 0)
        x = x + jnp.where(z_hi, pltpu.roll(up, 7, 1), 0.0) + jnp.where(z_lo, pltpu.roll(down, 121, 1), 0.0)
        up = jnp.concatenate([x[EZ:], x[:EZ]], 0)
        down = jnp.concatenate([x[ne - EZ:], x[: ne - EZ]], 0)
        return x + jnp.where(y_hi, pltpu.roll(up, 56, 1), 0.0) + jnp.where(y_lo, pltpu.roll(down, 72, 1), 0.0)

    flag_row = jnp.broadcast_to(act[...].astype(F32), (ne, ne))
    diag = lax.broadcasted_iota(jnp.int32, (ne, ne), 0) == lax.broadcasted_iota(jnp.int32, (ne, ne), 1)
    mask = jnp.dot(
        jnp.where(diag, flag_row, 0.0).astype(BF16), jnp.ones((ne, 128), BF16), preferred_element_type=F32
    )
    sym = [[(gram[f, h] + gram[h, f]) * 0.5 for h in range(nf)] for f in range(nf)]

    l_spread.wait()
    wts = spread[0:8, 1536:2048]
    build_tables(spread, fa, fbc, ba, bbc, bfa, bfbc)
    l_fld.wait()
    t_acc = jnp.zeros((8, 128), F32)
    b_acc = jnp.zeros((8, 128), F32)
    for ct in range(4):
        cols = slice(ct * 128, ct * 128 + 128)
        u = [fld[f * ne:(f + 1) * ne, cols].astype(F32) for f in range(nf)]
        square = sum(x * x for x in u)
        quad = 0.0
        for f in range(nf):
            inner = sym[f][f] * u[f]
            for h in range(f + 1, nf):
                inner = inner + (2.0 * sym[f][h]) * u[h]
            quad = quad + u[f] * inner
        mw = mask * wts[0:1, cols]
        t_acc = t_acc + jnp.sum((mw * square).reshape(ne // 8, 8, 128), 0)
        b_acc = b_acc + jnp.sum((mw * quad).reshape(ne // 8, 8, 128), 0)
    t_row = jnp.sum(t_acc, 0, keepdims=True)
    b_row = jnp.sum(b_acc, 0, keepdims=True)
    left = lax.broadcasted_iota(jnp.int32, (1, 128), 1) < 64
    part[...] = jnp.where(left, t_row, b_row) + pltpu.roll(jnp.where(left, b_row, t_row), 64, 1)

    pl.semaphore_wait(barrier, n - 1)

    @pl.loop(1, n)
    def _(o):
        pltpu.make_async_remote_copy(
            src_ref=part, dst_ref=parts.at[o - 1], send_sem=psend.at[o - 1], recv_sem=precv.at[o - 1],
            device_id={"gx": lax.rem(me + o, n)}, device_id_type=pl.DeviceIdType.MESH,
        ).start()

    def face_copy(slot):
        target = me - 1 if slot % 2 == 0 else me + 1
        there = slot + 1 if slot % 2 == 0 else slot - 1
        return pltpu.make_async_remote_copy(
            src_ref=sbuf.at[slot], dst_ref=rbuf.at[there], send_sem=fsend.at[slot], recv_sem=frecv.at[there],
            device_id={"gx": target}, device_id_type=pl.DeviceIdType.MESH,
        )

    def pack(face, slot):
        a, b = face[:half], face[half:]
        sbuf[slot] = jnp.where(low_half, a, pltpu.roll(b, 64, 1))
        sbuf[slot + 1] = jnp.where(low_half, pltpu.roll(a, 64, 1), b)

        @pl.when(me > 0)
        def _():
            face_copy(slot).start()

        @pl.when(me < n - 1)
        def _():
            face_copy(slot + 1).start()

    def unpack(slot):
        p, q = rbuf[slot], rbuf[slot + 1]
        return jnp.concatenate(
            [jnp.where(low_half, p, pltpu.roll(q, 64, 1)), jnp.where(low_half, pltpu.roll(p, 64, 1), q)], 0
        )

    def done(slot):
        @pl.when(me > 0)
        def _():
            face_copy(slot).wait_send()
            pltpu.make_async_copy(rbuf.at[slot], rbuf.at[slot], frecv.at[slot]).wait()

        @pl.when(me < n - 1)
        def _():
            face_copy(slot + 1).wait_send()
            pltpu.make_async_copy(rbuf.at[slot + 1], rbuf.at[slot + 1], frecv.at[slot + 1]).wait()

    pack(
        jnp.concatenate(
            [
                plane_sum(
                    mask
                    * jnp.where(
                        low, fld[f * ne:(f + 1) * ne, 0:128].astype(F32), fld[f * ne:(f + 1) * ne, 384:512].astype(F32)
                    )
                )
                for f in range(nf)
            ],
            0,
        ),
        0,
    )

    l_lam.wait()
    for f in range(nf):
        rs = slice(f * ne, (f + 1) * ne)
        lw[rs] = -wts[0:1] * lam[rs].astype(F32)
    l_vel.wait()
    for d in range(3):
        for t in range(2):
            cols = slice(t * 256, t * 256 + 256)
            if d == 0:
                grad = jnp.dot(lam[...], fa[:, cols], preferred_element_type=F32)
            else:
                grad = jnp.dot(lam[:, cols], fbc[:, (d - 1) * 256:d * 256], preferred_element_type=F32)
            flow = vel[d * ne:(d + 1) * ne, cols].astype(F32)
            for f in range(nf):
                rs = slice(f * ne, (f + 1) * ne)
                flux = (lw[rs, cols] * flow - (diff[f] * wts[0:1, cols]) * grad[rs]).astype(BF16)
                if d == 0:
                    q0[rs, cols] = flux
                else:
                    qbc[t, rs, (d - 1) * 256:d * 256] = flux

    low_rows = lax.broadcasted_iota(jnp.int32, (rows, 128), 1) < 64
    q1f = jnp.where(low_rows, qbc[0, :, 0:128], qbc[1, :, 128:256])
    q2f = jnp.where(low_rows, qbc[0, :, 256:384], qbc[1, :, 384:512])
    face = jnp.dot(q0[...], bfa[...], preferred_element_type=F32) + jnp.dot(
        jnp.concatenate([q1f, q2f], 1), bfbc[...], preferred_element_type=F32
    )
    pack(jnp.concatenate([plane_sum(mask * face[f * ne:(f + 1) * ne]) for f in range(nf)], 0), 2)

    for t in range(2):
        cols = slice(t * 256, t * 256 + 256)
        back = jnp.dot(q0[...], ba[:, cols], preferred_element_type=F32) + jnp.dot(
            qbc[t], bbc[...], preferred_element_type=F32
        )
        for s in range(2):
            ct = slice(t * 256 + s * 128, t * 256 + s * 128 + 128)
            for f in range(nf):
                rs = slice(f * ne, (f + 1) * ne)
                base[rs, ct] = mask * plane_sum(mask * back[rs, s * 128:s * 128 + 128])
    for ct in range(4):
        cols = slice(ct * 128, ct * 128 + 128)
        mw = mask * wts[0:1, cols]
        u = [mw * plane_sum(mask * fld[f * ne:(f + 1) * ne, cols].astype(F32)) for f in range(nf)]
        for f in range(nf):
            rs = slice(f * ne, (f + 1) * ne)
            plain[rs, cols] = u[f]
            mixed[rs, cols] = sum(sym[f][h] * u[h] for h in range(nf))

    done(0)
    got = unpack(0)
    wf = mask * jnp.where(low, wts[0:1, 0:128], wts[0:1, 384:512])
    u = [wf * got[f * ne:(f + 1) * ne] for f in range(nf)]
    for f in range(nf):
        rs = slice(f * ne, (f + 1) * ne)
        ends[0, rs] = u[f]
        ends[1, rs] = sum(sym[f][h] * u[h] for h in range(nf))

    for o in range(1, n):
        copy = pltpu.make_async_remote_copy(
            src_ref=part, dst_ref=parts.at[o - 1], send_sem=psend.at[o - 1], recv_sem=precv.at[o - 1],
            device_id={"gx": lax.rem(me + o, n)}, device_id_type=pl.DeviceIdType.MESH,
        )
        copy.wait()
    total = part[...]
    for o in range(1, n):
        total = total + parts[o - 1]
    trace = jnp.sum(jnp.where(left, total, 0.0), keepdims=True)
    beta = jnp.sum(jnp.where(left, 0.0, total), keepdims=True)
    c1 = jnp.broadcast_to(2.0 / trace, (1, 128))
    c2 = jnp.broadcast_to(-2.0 * beta / (trace * trace), (1, 128))
    for f in range(nf):
        rs = slice(f * ne, (f + 1) * ne)
        end = c1 * ends[1, rs] + c2 * ends[0, rs]
        for ct in range(4):
            cols = slice(ct * 128, ct * 128 + 128)
            value = base[rs, cols] + c1 * mixed[rs, cols] + c2 * plain[rs, cols]
            if ct == 0:
                value = value + jnp.where(low, end, 0.0)
            if ct == 3:
                value = value + jnp.where(low, 0.0, end)
            out[rs, cols] = value
    done(2)
    got = unpack(2)
    for f in range(nf):
        rs = slice(f * ne, (f + 1) * ne)
        end = mask * got[rs]
        out[rs, 0:128] = out[rs, 0:128] + jnp.where(low, end, 0.0)
        out[rs, 384:512] = out[rs, 384:512] + jnp.where(low, 0.0, end)


def per_device(n, fields, adjoint_seed, velocity, activity, diffusivity, gram_cotangent):
    nf, _, ne, nn = fields.shape
    rows = nf * ne
    table_shapes = ((nn, nn), (256, 512), (nn, nn), (512, 256), (nn, 128), (256, 128))
    vmem, anywhere = pl.BlockSpec(memory_space=pltpu.VMEM), pl.BlockSpec(memory_space=pltpu.HBM)
    smem = pl.BlockSpec(memory_space=pltpu.SMEM)
    result = pl.pallas_call(
        functools.partial(kernel, n, nf, ne),
        out_shape=pltpu.VMEM((rows, nn), F32),
        in_specs=[smem, smem, vmem] + [anywhere] * 4,
        out_specs=vmem,
        scratch_shapes=[
            pltpu.VMEM((rows, nn), BF16),
            pltpu.VMEM((rows, nn), BF16),
            pltpu.VMEM((3 * ne, nn), BF16),
            *[pltpu.VMEM(t, BF16) for t in table_shapes],
            pltpu.VMEM((8, 1536 + nn), F32),
            pltpu.VMEM((rows, nn), F32),
            pltpu.VMEM((rows, nn), BF16),
            pltpu.VMEM((2, rows, nn), BF16),
            pltpu.VMEM((rows, nn), F32),
            pltpu.VMEM((rows, nn), F32),
            pltpu.VMEM((rows, nn), F32),
            pltpu.VMEM((2, rows, 128), F32),
            pltpu.VMEM((1, 128), F32),
            pltpu.VMEM((n - 1, 1, 128), F32),
            pltpu.VMEM((4, rows // 2, 128), F32),
            pltpu.VMEM((4, rows // 2, 128), F32),
            pltpu.SemaphoreType.DMA((4,)),
            pltpu.SemaphoreType.DMA((n - 1,)),
            pltpu.SemaphoreType.DMA((n - 1,)),
            pltpu.SemaphoreType.DMA((4,)),
            pltpu.SemaphoreType.DMA((4,)),
        ],
        compiler_params=pltpu.CompilerParams(
            collective_id=0, has_side_effects=True, vmem_limit_bytes=60 * 1024 * 1024
        ),
    )(
        diffusivity,
        gram_cotangent,
        activity,
        fields.reshape(rows, nn),
        adjoint_seed.reshape(rows, nn),
        velocity.reshape(3 * ne, nn),
        jnp.asarray(constants()),
    )
    return result.reshape(nf, 1, ne, nn)


def solution(mesh):
    spec = P(None, ("member", "gx"), None, None)
    return jax.shard_map(
        functools.partial(per_device, mesh.shape["gx"]),
        mesh=mesh,
        in_specs=(spec, spec, spec, P(("member", "gx"), None), P(), P()),
        out_specs=spec,
        check_vma=False,
    )
```

```python
import functools
import jax
import jax.numpy as jnp
import ml_dtypes
import numpy as np
from jax import lax
from jax.experimental import pallas as pl
from jax.experimental.pallas import tpu as pltpu
from jax.sharding import PartitionSpec as P

EY = 4
EZ = 16
F32 = jnp.float32
BF16 = jnp.bfloat16


def basis_tables():
    degree = 7
    gll_points = np.array(
        [
            -1.0,
            -0.8717401485096066,
            -0.5917001814331423,
            -0.2092992179024789,
            0.2092992179024789,
            0.5917001814331423,
            0.8717401485096066,
            1.0,
        ]
    )
    prev_poly = np.ones(8)
    this_poly = gll_points.copy()
    for level in range(1, degree):
        prev_poly, this_poly = (
            this_poly,
            ((2 * level + 1) * gll_points * this_poly - level * prev_poly) / (level + 1),
        )
    gll_weights = 2.0 / (degree * (degree + 1) * this_poly**2)
    deriv = np.zeros((8, 8))
    for row_index in range(8):
        for col_index in range(8):
            if row_index != col_index:
                deriv[row_index, col_index] = this_poly[row_index] / (
                    this_poly[col_index] * (gll_points[row_index] - gll_points[col_index])
                )
    deriv[0, 0] = -degree * (degree + 1) / 4.0
    deriv[7, 7] = degree * (degree + 1) / 4.0
    weight_cube = (
        gll_weights[:, None, None] * gll_weights[None, :, None] * gll_weights[None, None, :]
    ).reshape(512)
    return (weight_cube, deriv)


def constants():
    weight_np, deriv_np = basis_tables()
    dmat = deriv_np.astype(np.float32).astype(ml_dtypes.bfloat16).astype(np.float32)
    lanes = np.arange(512)
    pieces = []
    for index in (lanes // 64, (lanes[:128] // 8) % 8, lanes[:128] % 8):
        pieces += [dmat[:, index], dmat.T[:, index]]
    pieces.append(np.broadcast_to(weight_np.astype(np.float32)[None], (8, 512)))
    return np.ascontiguousarray(np.concatenate(pieces, 1).astype(np.float32))


def build_tables(spread, fa, fbc, ba, bbc, bfa, bfbc):
    row64 = lax.broadcasted_iota(jnp.int32, (64, 512), 0)
    lane64 = lax.broadcasted_iota(jnp.int32, (64, 512), 1) & 63
    same = row64 == lane64
    low = lax.broadcasted_iota(jnp.int32, (64, 128), 1) < 64
    for p in range(8):
        rs = slice(p * 64, p * 64 + 64)
        plain = jnp.where(same, spread[p:p + 1, 0:512], 0.0).astype(BF16)
        ba[rs] = plain
        bfa[rs] = jnp.where(low, plain[:, 0:128], plain[:, 384:512])
        fa[rs] = jnp.where(same, spread[p:p + 1, 512:1024], 0.0).astype(BF16)
    row = lax.broadcasted_iota(jnp.int32, (128, 128), 0)
    lane = lax.broadcasted_iota(jnp.int32, (128, 128), 1)
    b_same = ((row & 7) == (lane & 7)) & ((row >> 6) == (lane >> 6))
    c_same = (row >> 3) == (lane >> 3)

    def b_table(at):
        rows = [jnp.broadcast_to(spread[g % 8:g % 8 + 1, at:at + 128], (8, 128)) for g in range(16)]
        return jnp.where(b_same, jnp.concatenate(rows, 0), 0.0).astype(BF16)

    def c_table(at):
        return jnp.where(c_same, jnp.concatenate([spread[:, at:at + 128]] * 16, 0), 0.0).astype(BF16)

    zero = jnp.zeros((128, 128), BF16)
    b, bt, c, ct = b_table(1024), b_table(1152), c_table(1280), c_table(1408)
    for k, (back, fwd) in enumerate(((b, bt), (c, ct))):
        fbc[0:128, k * 256:k * 256 + 256] = jnp.concatenate([fwd, zero], 1)
        fbc[128:256, k * 256:k * 256 + 256] = jnp.concatenate([zero, fwd], 1)
        bbc[k * 256:k * 256 + 128] = jnp.concatenate([back, zero], 1)
        bbc[k * 256 + 128:k * 256 + 256] = jnp.concatenate([zero, back], 1)
        bfbc[k * 128:k * 128 + 128] = back


def kernel(
    n, nf, ne,
    diff_hbm, gram_hbm, act_hbm, fld_hbm, lam_hbm, vel_hbm, spread_hbm,
    out,
    fld, lam, vel, fa, fbc, ba, bbc, bfa, bfbc, spread, diff, gram, act,
    lw, q0, qbc, base, mixed, plain, ends,
    part, parts, sbuf, rbuf,
    in_sem, psend, precv, fsend, frecv,
):
    me = lax.axis_index("gx")
    rows = nf * ne
    half = rows // 2

    pairs = (
        (act_hbm, act), (gram_hbm, gram), (diff_hbm, diff), (spread_hbm, spread), (fld_hbm, fld), (lam_hbm, lam), (vel_hbm, vel),
    )
    loads = [pltpu.make_async_copy(s, d, in_sem.at[i]) for i, (s, d) in enumerate(pairs)]
    for load in loads:
        load.start()
    l_act, l_gram, l_diff, l_spread, l_fld, l_lam, l_vel = loads

    barrier = pltpu.get_barrier_semaphore()

    @pl.loop(1, n)
    def _(o):
        pl.semaphore_signal(barrier, inc=1, device_id={"gx": lax.rem(me + o, n)}, device_id_type=pl.DeviceIdType.MESH)

    @pl.when(me == 0)
    def _():
        rbuf[0] = jnp.zeros((half, 128), F32)
        rbuf[2] = jnp.zeros((half, 128), F32)

    @pl.when(me == n - 1)
    def _():
        rbuf[1] = jnp.zeros((half, 128), F32)
        rbuf[3] = jnp.zeros((half, 128), F32)

    row = lax.broadcasted_iota(jnp.int32, (ne, 128), 0)
    lane = lax.broadcasted_iota(jnp.int32, (ne, 128), 1)
    low = lane < 64
    low_half = lax.broadcasted_iota(jnp.int32, (half, 128), 1) < 64
    c_id, b_id = lane & 7, (lane >> 3) & 7
    j_id, k_id = row >> 4, row & 15
    z_hi = (c_id == 7) & (k_id < EZ - 1)
    z_lo = (c_id == 0) & (k_id > 0)
    y_hi = (b_id == 7) & (j_id < EY - 1)
    y_lo = (b_id == 0) & (j_id > 0)

    def plane_sum(x):
        up, down = pltpu.roll(x, ne - 1, 0), pltpu.roll(x, 1, 0)
        x = x + jnp.where(z_hi, pltpu.roll(up, 7, 1), 0.0) + jnp.where(z_lo, pltpu.roll(down, 121, 1), 0.0)
        up = jnp.concatenate([x[EZ:], x[:EZ]], 0)
        down = jnp.concatenate([x[ne - EZ:], x[: ne - EZ]], 0)
        return x + jnp.where(y_hi, pltpu.roll(up, 56, 1), 0.0) + jnp.where(y_lo, pltpu.roll(down, 72, 1), 0.0)

    l_act.wait()
    l_gram.wait()
    l_diff.wait()
    flag_row = jnp.broadcast_to(act[...].astype(F32), (ne, ne))
    diag = lax.broadcasted_iota(jnp.int32, (ne, ne), 0) == lax.broadcasted_iota(jnp.int32, (ne, ne), 1)
    mask = jnp.dot(
        jnp.where(diag, flag_row, 0.0).astype(BF16), jnp.ones((ne, 128), BF16), preferred_element_type=F32
    )
    sym = [[(gram[f, h] + gram[h, f]) * 0.5 for h in range(nf)] for f in range(nf)]

    l_spread.wait()
    wts = spread[0:8, 1536:2048]
    build_tables(spread, fa, fbc, ba, bbc, bfa, bfbc)
    l_fld.wait()
    t_acc = jnp.zeros((8, 128), F32)
    b_acc = jnp.zeros((8, 128), F32)
    for ct in range(4):
        cols = slice(ct * 128, ct * 128 + 128)
        u = [fld[f * ne:(f + 1) * ne, cols].astype(F32) for f in range(nf)]
        square = sum(x * x for x in u)
        quad = 0.0
        for f in range(nf):
            inner = sym[f][f] * u[f]
            for h in range(f + 1, nf):
                inner = inner + (2.0 * sym[f][h]) * u[h]
            quad = quad + u[f] * inner
        mw = mask * wts[0:1, cols]
        t_acc = t_acc + jnp.sum((mw * square).reshape(ne // 8, 8, 128), 0)
        b_acc = b_acc + jnp.sum((mw * quad).reshape(ne // 8, 8, 128), 0)
    t_row = jnp.sum(t_acc, 0, keepdims=True)
    b_row = jnp.sum(b_acc, 0, keepdims=True)
    left = lax.broadcasted_iota(jnp.int32, (1, 128), 1) < 64
    part[...] = jnp.where(left, t_row, b_row) + pltpu.roll(jnp.where(left, b_row, t_row), 64, 1)

    pl.semaphore_wait(barrier, n - 1)

    @pl.loop(1, n)
    def _(o):
        pltpu.make_async_remote_copy(
            src_ref=part, dst_ref=parts.at[o - 1], send_sem=psend.at[o - 1], recv_sem=precv.at[o - 1],
            device_id={"gx": lax.rem(me + o, n)}, device_id_type=pl.DeviceIdType.MESH,
        ).start()

    def face_copy(slot):
        target = me - 1 if slot % 2 == 0 else me + 1
        there = slot + 1 if slot % 2 == 0 else slot - 1
        return pltpu.make_async_remote_copy(
            src_ref=sbuf.at[slot], dst_ref=rbuf.at[there], send_sem=fsend.at[slot], recv_sem=frecv.at[there],
            device_id={"gx": target}, device_id_type=pl.DeviceIdType.MESH,
        )

    def pack(face, slot):
        a, b = face[:half], face[half:]
        sbuf[slot] = jnp.where(low_half, a, pltpu.roll(b, 64, 1))
        sbuf[slot + 1] = jnp.where(low_half, pltpu.roll(a, 64, 1), b)

        @pl.when(me > 0)
        def _():
            face_copy(slot).start()

        @pl.when(me < n - 1)
        def _():
            face_copy(slot + 1).start()

    def unpack(slot):
        p, q = rbuf[slot], rbuf[slot + 1]
        return jnp.concatenate(
            [jnp.where(low_half, p, pltpu.roll(q, 64, 1)), jnp.where(low_half, pltpu.roll(p, 64, 1), q)], 0
        )

    def done(slot):
        @pl.when(me > 0)
        def _():
            face_copy(slot).wait_send()
            pltpu.make_async_copy(rbuf.at[slot], rbuf.at[slot], frecv.at[slot]).wait()

        @pl.when(me < n - 1)
        def _():
            face_copy(slot + 1).wait_send()
            pltpu.make_async_copy(rbuf.at[slot + 1], rbuf.at[slot + 1], frecv.at[slot + 1]).wait()

    pack(
        jnp.concatenate(
            [
                plane_sum(
                    mask
                    * jnp.where(
                        low, fld[f * ne:(f + 1) * ne, 0:128].astype(F32), fld[f * ne:(f + 1) * ne, 384:512].astype(F32)
                    )
                )
                for f in range(nf)
            ],
            0,
        ),
        0,
    )

    l_lam.wait()
    for f in range(nf):
        rs = slice(f * ne, (f + 1) * ne)
        lw[rs] = -wts[0:1] * lam[rs].astype(F32)
    l_vel.wait()
    for d in range(3):
        for t in range(2):
            cols = slice(t * 256, t * 256 + 256)
            if d == 0:
                grad = jnp.dot(lam[...], fa[:, cols], preferred_element_type=F32)
            else:
                grad = jnp.dot(lam[:, cols], fbc[:, (d - 1) * 256:d * 256], preferred_element_type=F32)
            flow = vel[d * ne:(d + 1) * ne, cols].astype(F32)
            for f in range(nf):
                rs = slice(f * ne, (f + 1) * ne)
                flux = (lw[rs, cols] * flow - (diff[f] * wts[0:1, cols]) * grad[rs]).astype(BF16)
                if d == 0:
                    q0[rs, cols] = flux
                else:
                    qbc[t, rs, (d - 1) * 256:d * 256] = flux

    low_rows = lax.broadcasted_iota(jnp.int32, (rows, 128), 1) < 64
    q1f = jnp.where(low_rows, qbc[0, :, 0:128], qbc[1, :, 128:256])
    q2f = jnp.where(low_rows, qbc[0, :, 256:384], qbc[1, :, 384:512])
    face = jnp.dot(q0[...], bfa[...], preferred_element_type=F32) + jnp.dot(
        jnp.concatenate([q1f, q2f], 1), bfbc[...], preferred_element_type=F32
    )
    pack(jnp.concatenate([plane_sum(mask * face[f * ne:(f + 1) * ne]) for f in range(nf)], 0), 2)

    for t in range(2):
        cols = slice(t * 256, t * 256 + 256)
        back = jnp.dot(q0[...], ba[:, cols], preferred_element_type=F32) + jnp.dot(
            qbc[t], bbc[...], preferred_element_type=F32
        )
        for s in range(2):
            ct = slice(t * 256 + s * 128, t * 256 + s * 128 + 128)
            for f in range(nf):
                rs = slice(f * ne, (f + 1) * ne)
                base[rs, ct] = mask * plane_sum(mask * back[rs, s * 128:s * 128 + 128])
    for ct in range(4):
        cols = slice(ct * 128, ct * 128 + 128)
        mw = mask * wts[0:1, cols]
        u = [mw * plane_sum(mask * fld[f * ne:(f + 1) * ne, cols].astype(F32)) for f in range(nf)]
        for f in range(nf):
            rs = slice(f * ne, (f + 1) * ne)
            plain[rs, cols] = u[f]
            mixed[rs, cols] = sum(sym[f][h] * u[h] for h in range(nf))

    done(0)
    got = unpack(0)
    wf = mask * jnp.where(low, wts[0:1, 0:128], wts[0:1, 384:512])
    u = [wf * got[f * ne:(f + 1) * ne] for f in range(nf)]
    for f in range(nf):
        rs = slice(f * ne, (f + 1) * ne)
        ends[0, rs] = u[f]
        ends[1, rs] = sum(sym[f][h] * u[h] for h in range(nf))

    for o in range(1, n):
        copy = pltpu.make_async_remote_copy(
            src_ref=part, dst_ref=parts.at[o - 1], send_sem=psend.at[o - 1], recv_sem=precv.at[o - 1],
            device_id={"gx": lax.rem(me + o, n)}, device_id_type=pl.DeviceIdType.MESH,
        )
        copy.wait()
    total = part[...]
    for o in range(1, n):
        total = total + parts[o - 1]
    trace = jnp.sum(jnp.where(left, total, 0.0), keepdims=True)
    beta = jnp.sum(jnp.where(left, 0.0, total), keepdims=True)
    c1 = jnp.broadcast_to(2.0 / trace, (1, 128))
    c2 = jnp.broadcast_to(-2.0 * beta / (trace * trace), (1, 128))
    for f in range(nf):
        rs = slice(f * ne, (f + 1) * ne)
        end = c1 * ends[1, rs] + c2 * ends[0, rs]
        for ct in range(4):
            cols = slice(ct * 128, ct * 128 + 128)
            value = base[rs, cols] + c1 * mixed[rs, cols] + c2 * plain[rs, cols]
            if ct == 0:
                value = value + jnp.where(low, end, 0.0)
            if ct == 3:
                value = value + jnp.where(low, 0.0, end)
            out[rs, cols] = value
    done(2)
    got = unpack(2)
    for f in range(nf):
        rs = slice(f * ne, (f + 1) * ne)
        end = mask * got[rs]
        out[rs, 0:128] = out[rs, 0:128] + jnp.where(low, end, 0.0)
        out[rs, 384:512] = out[rs, 384:512] + jnp.where(low, 0.0, end)


def per_device(n, fields, adjoint_seed, velocity, activity, diffusivity, gram_cotangent):
    nf, _, ne, nn = fields.shape
    rows = nf * ne
    table_shapes = ((nn, nn), (256, 512), (nn, nn), (512, 256), (nn, 128), (256, 128))
    vmem, anywhere = pl.BlockSpec(memory_space=pltpu.VMEM), pl.BlockSpec(memory_space=pltpu.HBM)
    result = pl.pallas_call(
        functools.partial(kernel, n, nf, ne),
        out_shape=pltpu.VMEM((rows, nn), F32),
        in_specs=[anywhere] * 7,
        out_specs=vmem,
        scratch_shapes=[
            pltpu.VMEM((rows, nn), BF16),
            pltpu.VMEM((rows, nn), BF16),
            pltpu.VMEM((3 * ne, nn), BF16),
            *[pltpu.VMEM(t, BF16) for t in table_shapes],
            pltpu.VMEM((8, 1536 + nn), F32),
            pltpu.SMEM(diffusivity.shape, F32),
            pltpu.SMEM(gram_cotangent.shape, F32),
            pltpu.VMEM(activity.shape, jnp.int32),
            pltpu.VMEM((rows, nn), F32),
            pltpu.VMEM((rows, nn), BF16),
            pltpu.VMEM((2, rows, nn), BF16),
            pltpu.VMEM((rows, nn), F32),
            pltpu.VMEM((rows, nn), F32),
            pltpu.VMEM((rows, nn), F32),
            pltpu.VMEM((2, rows, 128), F32),
            pltpu.VMEM((1, 128), F32),
            pltpu.VMEM((n - 1, 1, 128), F32),
            pltpu.VMEM((4, rows // 2, 128), F32),
            pltpu.VMEM((4, rows // 2, 128), F32),
            pltpu.SemaphoreType.DMA((7,)),
            pltpu.SemaphoreType.DMA((n - 1,)),
            pltpu.SemaphoreType.DMA((n - 1,)),
            pltpu.SemaphoreType.DMA((4,)),
            pltpu.SemaphoreType.DMA((4,)),
        ],
        compiler_params=pltpu.CompilerParams(
            collective_id=0, has_side_effects=True, vmem_limit_bytes=60 * 1024 * 1024
        ),
    )(
        diffusivity,
        gram_cotangent,
        activity,
        fields.reshape(rows, nn),
        adjoint_seed.reshape(rows, nn),
        velocity.reshape(3 * ne, nn),
        jnp.asarray(constants()),
    )
    return result.reshape(nf, 1, ne, nn)


def solution(mesh):
    spec = P(None, ("member", "gx"), None, None)
    return jax.shard_map(
        functools.partial(per_device, mesh.shape["gx"]),
        mesh=mesh,
        in_specs=(spec, spec, spec, P(("member", "gx"), None), P(), P()),
        out_specs=spec,
        check_vma=False,
    )
```
